32 devices in a mesh: shard: 2 (over x), ctx: 4 (over y, core), tp: 4 (over z).
Axes of the slice: x: 2, y: 2, z: 4, core: 2. Of those that a mesh axis runs over, the one named last changes fastest.
Arguments:
- hidden_in: bfloat16 [2, 768, 1024], P('shard', 'ctx'), may hold values from -6 to 6
- seg_ids: int32 [2, 768], P('shard'), may hold values from 0 to 3, as said below
- attn_in: bfloat16 [2, 3, 1024, 1024], P(None, None, ('shard', 'ctx'), 'tp'), may hold values from -0.1875 to 0.1875
- attn_bias: bfloat16 [2, 2, 4, 256], P(None, None, 'tp', ('shard', 'ctx')), may hold values from -3 to 3
- attn_out: bfloat16 [2, 1024, 1024], P(None, 'tp', ('shard', 'ctx')), may hold values from -0.75 to 0.75
- ff_in: bfloat16 [2, 1024, 4096], P(None, ('shard', 'ctx'), 'tp'), may hold values from -0.1875 to 0.1875
- ff_bias: bfloat16 [2, 4, 1024], P(None, 'tp', ('shard', 'ctx')), may hold values from -3 to 3
- ff_out: bfloat16 [2, 4096, 1024], P(None, 'tp', ('shard', 'ctx')), may hold values from -0.09375 to 0.09375
- gains: bfloat16 [2, 2, 1024], P(None, None, ('shard', 'ctx')), may hold values from 0.5 to 1.5
- shifts: bfloat16 [2, 4, 1024], P(None, None, ('shard', 'ctx')), may hold values from -3 to 3
- cotangent: bfloat16 [2, 768, 1024], P('shard', 'ctx'), may hold values from -6 to 6
Outputs:
- hidden_out: bfloat16 [2, 768, 1024], P('shard', 'ctx')
- grad_in: float32 [2, 768, 1024], P('shard', 'ctx')
- grad_attn_in: float32 [2, 3, 1024, 1024], P(None, None, ('shard', 'ctx'), 'tp')
- grad_attn_bias: float32 [2, 2, 4, 256], P(None, None, 'tp', ('shard', 'ctx'))
- grad_attn_out: float32 [2, 1024, 1024], P(None, 'tp', ('shard', 'ctx'))
- grad_ff_in: float32 [2, 1024, 4096], P(None, ('shard', 'ctx'), 'tp')
- grad_ff_bias: float32 [2, 4, 1024], P(None, 'tp', ('shard', 'ctx'))
- grad_ff_out: float32 [2, 4096, 1024], P(None, 'tp', ('shard', 'ctx'))
- grad_gains: float32 [2, 2, 1024], P(None, None, ('shard', 'ctx'))
- grad_shifts: float32 [2, 4, 1024], P(None, None, ('shard', 'ctx'))
The draws below stay inside these ranges and needn't reach their ends.
Inputs may be any that keep to these rules, and one draw needn't show every extreme that they name: `seg_ids`: each row holds four sequences numbered 0 to 3 in order, each at least one position long; sequence 1 holds exactly 512 positions and reaches from the first 192 positions of its row into the last 192.
All inputs are finite; a program needn't handle non-finite values.
Results may differ from the reference program's by a relative error of at most 0.02.
Values may be sent and summed in bfloat16 or wider, within the bound.
No kernel may reach another device: no remote copies, remote signals or barrier semaphores. Data moves between devices by JAX's collectives and lax.ppermute only.
A program may use at most 128 MiB of HBM per device.

```python
import jax
import jax.numpy as jnp
from jax import lax

D = 1024
HEADS = 16
HD = 64
FF = 4096
LAYERS = 2
LONGEST = 512
TOK_DEV = 192
PACK_LEN = 768
PACKS = 2
N_TP = 4


def pack_segments(pack_key):
    first_key, cut_key = jax.random.split(pack_key)
    lowest = max(1, PACK_LEN - TOK_DEV - LONGEST + 1)
    opening = jax.random.randint(first_key, (), lowest, TOK_DEV).astype(jnp.int32)
    remainder = PACK_LEN - opening - LONGEST
    cut_place = opening + LONGEST + jax.random.randint(cut_key, (), 1, remainder).astype(jnp.int32)
    positions = jnp.arange(PACK_LEN, dtype=jnp.int32)
    first_mark = (positions >= opening).astype(jnp.int32)
    second_mark = (positions >= opening + LONGEST).astype(jnp.int32)
    third_mark = (positions >= cut_place).astype(jnp.int32)
    return first_mark + second_mark + third_mark


def draw_seg_ids(key, part):
    key = jax.random.fold_in(key, 5)
    pack_keys = jax.random.split(key, PACKS)
    return jax.vmap(pack_segments)(pack_keys).astype(jnp.int32)


def steps_of(rng, shape, cuts, low, top_value):
    level = 1.0
    for position, blocks in cuts:
        steps = jax.random.uniform(jax.random.fold_in(jax.random.fold_in(rng, 6), position), (blocks,), jnp.float32, low / len(cuts), top_value / len(cuts))
        level = level * jnp.repeat(jnp.exp(steps), shape[position] // blocks).reshape((-1,) + (1,) * (len(shape) - 1 - position))
    return level


def scatter_about(own_key, shape, deviation, bound, cuts=(), kind=jnp.bfloat16):
    entries = jax.random.normal(own_key, shape, jnp.float32) * deviation
    if len(cuts) > 0:
        entries = steps_of(own_key, shape, cuts, -0.22, 0.18) * entries
    return jnp.clip(entries, min=-bound, max=bound).astype(kind)


def setup_inputs(seed: int = 0) -> dict:
    key_list = jax.random.split(jax.random.key(seed), 12)
    return {
        "hidden_in": scatter_about(key_list[0], (PACKS, PACK_LEN, D), 1.0, 6.0, ((0, 2), (1, 4))),
        "seg_ids": draw_seg_ids(jax.random.fold_in(key_list[11], 71), 0),
        "attn_in": scatter_about(key_list[2], (LAYERS, 3, D, D), D ** -0.5, 0.1875, ((2, 8), (3, 4))),
        "attn_bias": scatter_about(key_list[3], (LAYERS, 2, N_TP, D // N_TP), 0.5, 3.0, ((2, 4), (3, 8))),
        "attn_out": scatter_about(key_list[4], (LAYERS, D, D), (D // 16) ** -0.5, 0.75, ((1, 4), (2, 8))),
        "ff_in": scatter_about(key_list[5], (LAYERS, D, FF), D ** -0.5, 0.1875, ((1, 8), (2, 4))),
        "ff_bias": scatter_about(key_list[6], (LAYERS, N_TP, FF // N_TP), 0.5, 3.0, ((1, 4), (2, 8))),
        "ff_out": scatter_about(key_list[7], (LAYERS, FF, D), FF ** -0.5, 0.09375, ((1, 4), (2, 8))),
        "gains": jnp.clip(1.0 + 0.1 * jax.random.normal(key_list[8], (LAYERS, 2, D), jnp.float32), 0.5, 1.5).astype(jnp.bfloat16),
        "shifts": scatter_about(key_list[9], (LAYERS, 4, D), 0.5, 3.0, ((2, 8),)),
        "cotangent": scatter_about(key_list[10], (PACKS, PACK_LEN, D), 1.0, 6.0, ((0, 2), (1, 4))),
    }


@jax.custom_vjp
def low(v):
    return lax.optimization_barrier(v.astype(jnp.bfloat16)).astype(jnp.float32)

@jax.custom_vjp
def low_back(v):
    return v

def low_keep(v):
    return (low(v), None)

def low_pass(kept, grad):
    return (grad,)

def back_keep(v):
    return (v, None)

def back_low(kept, grad):
    return (low(grad),)
low.defvjp(low_keep, low_pass)
low_back.defvjp(back_keep, back_low)

def matmul_high(left, right):
    return jnp.matmul(left, right, precision=lax.Precision.HIGHEST)

def layer_norm(values, gain, shift):
    centre = values - lax.optimization_barrier(jnp.mean(values, axis=-1, keepdims=True))
    inverse = lax.rsqrt(lax.optimization_barrier(jnp.mean(centre * centre, axis=-1, keepdims=True)) + 1e-12)
    return centre * inverse * gain + shift

def one_layer(inputs, same_seq, params):
    w_qkv, bias_qv, w_out, w_up, bias_up, w_down, gain_pair, shift_four = params
    length = inputs.shape[0]
    inputs_low = low(inputs)
    bias_flat = bias_qv.reshape(2, -1)
    queries = low_back(low(matmul_high(inputs_low, w_qkv[0]) + bias_flat[0]))
    keys_all = low_back(low(matmul_high(inputs_low, w_qkv[1])))
    values_all = low_back(low(matmul_high(inputs_low, w_qkv[2]) + bias_flat[1]))
    query_heads = queries.reshape(length, HEADS, HD)
    key_heads = keys_all.reshape(length, HEADS, HD)
    value_heads = values_all.reshape(length, HEADS, HD)
    scores = low_back(jnp.einsum('qhd,khd->hqk', query_heads, key_heads, precision=lax.Precision.HIGHEST) * HD ** (-0.5))
    scores = jnp.where(same_seq[None], scores, -1e+30)
    top_score = lax.optimization_barrier(jnp.max(scores, axis=-1, keepdims=True))
    exponent = jnp.exp(scores - top_score)
    prob_table = low(exponent / lax.optimization_barrier(jnp.sum(exponent, axis=-1, keepdims=True)))
    context = jnp.einsum('hqk,khd->qhd', prob_table, value_heads, precision=lax.Precision.HIGHEST)
    context = low_back(low(context.reshape(length, HEADS * HD)))
    attn_output = low_back(matmul_high(context, w_out)) + shift_four[0]
    hidden = layer_norm(inputs + attn_output, gain_pair[0], shift_four[1])
    up_proj = low_back(matmul_high(low(hidden), w_up) + bias_up.reshape(-1))
    active = low(jax.nn.gelu(up_proj, approximate=False))
    ff_output = low_back(matmul_high(active, w_down)) + shift_four[2]
    return layer_norm(hidden + ff_output, gain_pair[1], shift_four[3])

def forward(rows_in, same_seq, params):
    attn_in, attn_bias, attn_out, ff_in, ff_bias, ff_out, gains, shifts = params
    current = rows_in
    for layer_index in range(LAYERS):
        layer_params = (attn_in[layer_index], attn_bias[layer_index], attn_out[layer_index], ff_in[layer_index], ff_bias[layer_index], ff_out[layer_index], gains[layer_index], shifts[layer_index])
        current = one_layer(current, same_seq, layer_params)
    return current

def reference(hidden_in, seg_ids, attn_in, attn_bias, attn_out, ff_in, ff_bias, ff_out, gains, shifts, cotangent):
    params = tuple((member.astype(jnp.float32) for member in (attn_in, attn_bias, attn_out, ff_in, ff_bias, ff_out, gains, shifts)))

    def per_pack(totals, packed):
        rows_in, segments, grad_rows = packed
        same_seq = segments[:, None] == segments[None, :]

        def run_forward(weights, inputs):
            return forward(inputs, same_seq, weights)
        output, pullback = jax.vjp(run_forward, params, rows_in.astype(jnp.float32))
        grad_params, grad_inputs = pullback(grad_rows.astype(jnp.float32))
        totals = jax.tree.map(jnp.add, totals, grad_params)
        return (totals, (output.astype(jnp.bfloat16), grad_inputs))
    start_sums = jax.tree.map(jnp.zeros_like, params)
    totals, (hidden_out, grad_in) = lax.scan(per_pack, start_sums, (hidden_in, seg_ids, cotangent))
    return (hidden_out, grad_in, totals[0], totals[1], totals[2], totals[3], totals[4], totals[5], totals[6], totals[7])
```

```python
import functools

import jax
import jax.numpy as jnp
from jax import lax
from jax.experimental import pallas as pl
from jax.experimental.pallas import tpu as pltpu
from jax.sharding import PartitionSpec as P

HD = 64
LANES = 128
SCORE_FLOOR = -1e30
PLANE = ("shard", "ctx")
BF = jnp.bfloat16
F32 = jnp.float32


def dot(left, right):
    return jnp.dot(left, right, preferred_element_type=F32)


def dot_nt(left, right):
    return lax.dot_general(left, right, (((1,), (1,)), ((), ())), preferred_element_type=F32)


def dot_tn(left, right):
    return lax.dot_general(left, right, (((0,), (0,)), ((), ())), preferred_element_type=F32)


def sds(shape, kind):
    return jax.ShapeDtypeStruct(shape, kind)


def whole():
    return pl.BlockSpec(memory_space=pltpu.VMEM)


def call(body, out_shape, in_specs, *operands, flops=0, name=None):
    moved = sum(o.size * o.dtype.itemsize for o in operands)
    moved += sum(o.size * o.dtype.itemsize for o in out_shape)
    return pl.pallas_call(
        body,
        out_shape=out_shape,
        in_specs=in_specs,
        out_specs=[whole() for _ in out_shape],
        compiler_params=pltpu.CompilerParams(vmem_limit_bytes=40 * 1024 * 1024),
        cost_estimate=pl.CostEstimate(flops=flops, bytes_accessed=moved, transcendentals=0),
        name=name,
    )(*operands)


def swap(value, axis, size, flip):
    return lax.ppermute(value, axis, [(i, i ^ flip) for i in range(size)])


def swap_all(pieces, axis, size):
    order = [k for k in (2, 3, 1) if k < size] + list(range(4, size))
    got = {k: swap(pieces[k], axis, size, k) for k in order}
    return [got[k] for k in range(1, size)]


def pick(blocks, index):
    return lax.dynamic_index_in_dim(blocks, index, 0, False)


def reorder(blocks, me):
    return jnp.stack([pick(blocks, me ^ k) for k in range(blocks.shape[0])])


def pack_in(matrix):
    c, rows, cols = matrix.shape
    return matrix.reshape(c, rows, cols // LANES, LANES).transpose(0, 2, 1, 3).reshape(-1, LANES)


def unpack_in(packed, c, rows, cols):
    return (
        packed.reshape(c, cols // LANES, rows, LANES).transpose(0, 2, 1, 3).reshape(c, rows, cols)
    )


def blocks_of_rows(matrix):
    c, depth, cols = matrix.shape
    cut = matrix.reshape(c, depth // LANES, LANES, cols // LANES, LANES)
    return cut.transpose(1, 0, 3, 2, 4).reshape(depth // LANES, -1, LANES)


def rows_of_blocks(packed, c, cols):
    blocks = packed.shape[0]
    cut = packed.reshape(blocks, c, cols // LANES, LANES, LANES)
    return cut.transpose(1, 0, 3, 2, 4).reshape(c, blocks * LANES, cols)


def blocks_of_cols(matrix):
    rows, width = matrix.shape
    return matrix.reshape(rows, width // LANES, LANES).transpose(1, 0, 2)


def cols_of_blocks(packed):
    blocks, rows, _ = packed.shape
    return packed.transpose(1, 0, 2).reshape(rows, blocks * LANES)


def gather_first(attn_in, smalls, shard_n, ctx_n, me, fast):
    if not fast:
        full = lax.all_gather(attn_in, PLANE, axis=1, tiled=True)
        rows = lax.all_gather(smalls, PLANE, axis=1, tiled=True)
        return blocks_of_rows(full), rows
    own = jnp.concatenate([pack_in(attn_in), smalls], axis=0)
    half = own.shape[0] // 2
    over_x = swap(own, "shard", 2, 1)
    over_y = swap(own, "ctx", 4, 2)
    across = jnp.concatenate(
        [swap(over_y[:half], "shard", 2, 1), swap(over_x[half:], "ctx", 4, 2)], axis=0
    )
    mine = jnp.stack([own, over_y, over_x, across])
    other = swap(mine, "ctx", 4, 1)
    both = jnp.stack([mine, other], axis=1).reshape(8, own.shape[0], LANES)
    natural = reorder(both, me)
    count = smalls.shape[0]
    small_rows = natural[:, -count:].transpose(1, 0, 2).reshape(count, -1)
    return natural[:, :-count], small_rows


def gather_in(attn_in, fast):
    if not fast:
        return blocks_of_rows(lax.all_gather(attn_in, PLANE, axis=1, tiled=True))
    return lax.all_gather(pack_in(attn_in), PLANE, axis=0, tiled=False)


def gather_rest(ff_in, ff_out, attn_out, fast):
    if not fast:
        up = lax.all_gather(ff_in, PLANE, axis=0, tiled=True)
        down = lax.all_gather(ff_out, PLANE, axis=1, tiled=True)
        out = lax.all_gather(attn_out, PLANE, axis=1, tiled=True)
        return jnp.concatenate(
            [blocks_of_rows(up[None]), blocks_of_cols(down), blocks_of_cols(out)], axis=1
        )
    own = jnp.concatenate([pack_in(ff_in[None]), ff_out, attn_out], axis=0)
    return lax.all_gather(own, PLANE, axis=0, tiled=False)


def scatter_ff(packed, hidden, fast):
    if not fast:
        up = rows_of_blocks(packed[:, :hidden], 1, hidden)[0]
        down = cols_of_blocks(packed[:, hidden:])
        return (
            lax.psum_scatter(up, PLANE, scatter_dimension=0, tiled=True).astype(F32),
            lax.psum_scatter(down, PLANE, scatter_dimension=1, tiled=True).astype(F32),
        )
    own = lax.psum_scatter(packed, PLANE, scatter_dimension=0, tiled=False)
    up = unpack_in(own[:hidden], 1, LANES, hidden)[0]
    return up.astype(F32), own[hidden:].astype(F32)


def scatter_attn(packed, width, fast):
    cut = packed.shape[1] - width
    if not fast:
        stack = rows_of_blocks(packed[:, :cut], 3, width)
        out = cols_of_blocks(packed[:, cut:])
        return (
            lax.psum_scatter(stack, PLANE, scatter_dimension=1, tiled=True).astype(F32),
            lax.psum_scatter(out, PLANE, scatter_dimension=1, tiled=True).astype(F32),
        )
    own = lax.psum_scatter(packed, PLANE, scatter_dimension=0, tiled=False)
    return unpack_in(own[:cut], 3, LANES, width).astype(F32), own[cut:].astype(F32)


def join(refs, target):
    step = refs[0].shape[0]
    for k, ref in enumerate(refs):
        target[k * step : (k + 1) * step, :] = ref[...]


def split_rows(value, refs, columns=slice(None)):
    step = refs[0].shape[0]
    for k, ref in enumerate(refs):
        ref[:, columns] = value[k * step : (k + 1) * step].astype(ref.dtype)


def in_matrix(w, c, halves):
    depth = w.shape[0] * LANES
    return jnp.concatenate(
        [
            w[:, (c * halves + h) * LANES : (c * halves + h + 1) * LANES, :].reshape(depth, LANES)
            for h in range(halves)
        ],
        axis=1,
    )


def up_pair(w, pair):
    depth = w.shape[0] * LANES
    return jnp.concatenate(
        [w[:, n * LANES : (n + 1) * LANES, :].reshape(depth, LANES) for n in (2 * pair, 2 * pair + 1)],
        axis=1,
    )


def down_pair(w, pair, first, count):
    return jnp.concatenate(
        [w[s, first : first + count, :] for s in (2 * pair, 2 * pair + 1)], axis=1
    )


def qkv_body(n, *refs):
    x_refs, (w, bias, x_out, q_out, kv_out) = refs[:n], refs[n:]
    join(x_refs, x_out)
    x = x_out[...]
    width = q_out.shape[1]
    halves = width // LANES
    q_out[...] = (dot(x, in_matrix(w, 0, halves)) + bias[0:1, :]).astype(BF)
    kv_out[:, :width] = dot(x, in_matrix(w, 1, halves)).astype(BF)
    kv_out[:, width:] = (dot(x, in_matrix(w, 2, halves)) + bias[1:2, :]).astype(BF)


def attend_body(m, n, *refs):
    q_ref, kv_refs = refs[0], refs[1 : 1 + m]
    seg_q, seg_k, w = refs[1 + m : 4 + m]
    o_out, lse_out, kv_all = refs[4 + m : 7 + m]
    pieces = refs[7 + m :]
    join(kv_refs, kv_all)
    width = q_ref.shape[1]
    same = seg_q[...] == seg_k[...]
    for h in range(width // HD):
        cols = slice(h * HD, (h + 1) * HD)
        vcols = slice(width + h * HD, width + (h + 1) * HD)
        s = dot_nt(q_ref[:, cols], kv_all[:, cols]) * HD ** (-0.5)
        s = jnp.where(same, s, SCORE_FLOOR)
        top = jnp.max(s, axis=-1, keepdims=True)
        e = jnp.exp(s - top)
        total = jnp.sum(e, axis=-1, keepdims=True)
        prob = (e / total).astype(BF)
        lse_out[:, h : h + 1] = top + jnp.log(total)
        o_out[:, cols] = dot(prob, kv_all[:, vcols]).astype(BF)
    o = o_out[...]
    for pair in range(w.shape[0] // 2):
        span = slice(2 * pair * LANES, (2 * pair + 2) * LANES)
        split_rows(dot(o, down_pair(w, pair, 0, width)), pieces, span)


def norm_body(n, *refs):
    base, own = refs[0], refs[1]
    others = refs[2 : 1 + n]
    shift, gain, centre_shift, out, out_low, normed, inverse = refs[1 + n :]
    r = base[...] + own[...]
    for other in others:
        r = r + other[...].astype(F32)
    r = r + shift[...]
    centre = r - jnp.mean(r, axis=-1, keepdims=True)
    inv = lax.rsqrt(jnp.mean(centre * centre, axis=-1, keepdims=True) + 1e-12)
    norm = centre * inv
    y = norm * gain[...] + centre_shift[...]
    out[...] = y
    out_low[...] = y.astype(BF)
    normed[...] = norm
    inverse[...] = jnp.broadcast_to(inv, inverse.shape)


def ff_body(n, *refs):
    h_refs = refs[:n]
    w, bias, h_out, slope_out, act_out = refs[n : n + 5]
    pieces = refs[n + 5 :]
    join(h_refs, h_out)
    h = h_out[...]
    hidden = act_out.shape[1]
    for pair in range(hidden // (2 * LANES)):
        span = slice(2 * pair * LANES, (2 * pair + 2) * LANES)
        u = dot(h, up_pair(w, pair)) + bias[:, span]
        cdf = 0.5 * (1.0 + lax.erf(u * (0.5**0.5)))
        act_out[:, span] = (u * cdf).astype(BF)
        slope_out[:, span] = cdf + u * (jnp.exp(-0.5 * u * u) * 0.3989422804014327)
    act = act_out[...]
    for pair in range(w.shape[0] // 2):
        span = slice(2 * pair * LANES, (2 * pair + 2) * LANES)
        split_rows(dot(act, down_pair(w, pair, hidden, hidden)), pieces, span)


def norm_back_body(n, *refs):
    base, own = refs[0], refs[1 : 2 if n else 1]
    others = refs[2 : 1 + n] if n else ()
    normed, inverse, gain, grad, grad_low, sums = refs[1 + n :]
    dy = base[...]
    for ref in own:
        dy = dy + ref[...]
    for ref in others:
        dy = dy + ref[...].astype(F32)
    norm = normed[...]
    e = dy * gain[...]
    dr = inverse[:, 0:1] * (
        e
        - jnp.mean(e, axis=-1, keepdims=True)
        - norm * jnp.mean(e * norm, axis=-1, keepdims=True)
    )
    grad[...] = dr
    grad_low[...] = dr.astype(BF)
    sums[...] = jnp.zeros_like(sums)
    sums[0:1, :] = jnp.sum(dy * norm, axis=0, keepdims=True)
    sums[1:2, :] = jnp.sum(dy, axis=0, keepdims=True)
    sums[2:3, :] = jnp.sum(dr, axis=0, keepdims=True)


def ff_back_body(n, *refs):
    g_refs = refs[:n]
    w, slope, g_out, du_out, bias_out = refs[n : n + 5]
    pieces = refs[n + 5 : 2 * n + 5]
    total = refs[2 * n + 5]
    join(g_refs, g_out)
    hidden = du_out.shape[1]
    for pair in range(w.shape[0] // 2):
        span = slice(2 * pair * LANES, (2 * pair + 2) * LANES)
        term = dot_nt(g_out[:, span], down_pair(w, pair, hidden, hidden))
        total[...] = term if pair == 0 else total[...] + term
    du = (total[...] * slope[...]).astype(BF)
    du_out[...] = du
    bias_out[...] = jnp.broadcast_to(
        jnp.sum(du.astype(F32), axis=0, keepdims=True), bias_out.shape
    )
    for pair in range(hidden // (2 * LANES)):
        span = slice(2 * pair * LANES, (2 * pair + 2) * LANES)
        term = dot_nt(du_out[:, span], up_pair(w, pair))
        total[...] = term if pair == 0 else total[...] + term
    split_rows(total[...], pieces)


def ff_grad_body(h_ref, act_ref, g_ref, du_ref, out):
    h, act = h_ref[...], act_ref[...]
    hidden = act.shape[1]
    blocks = out.shape[0]
    for pair in range(hidden // (2 * LANES)):
        span = slice(2 * pair * LANES, (2 * pair + 2) * LANES)
        grad = dot_tn(h, du_ref[:, span]).astype(BF).reshape(blocks, LANES, 2 * LANES)
        for j in range(2):
            n = 2 * pair + j
            out[:, n * LANES : (n + 1) * LANES, :] = grad[:, :, j * LANES : (j + 1) * LANES]
    for pair in range(blocks // 2):
        span = slice(2 * pair * LANES, (2 * pair + 2) * LANES)
        grad = dot_tn(act, g_ref[:, span]).astype(BF)
        for j in range(2):
            out[2 * pair + j, hidden : 2 * hidden, :] = grad[:, j * LANES : (j + 1) * LANES]


def attend_back_body(n, m, *refs):
    g_refs = refs[:n]
    w, q_ref, kv, lse, seg_q, seg_k, g_out, dq_out, near_out, far_out, do_ref, grads = refs[n:]
    join(g_refs, g_out)
    width = q_ref.shape[1]
    scale = HD ** (-0.5)
    for pair in range(w.shape[0] // 2):
        span = slice(2 * pair * LANES, (2 * pair + 2) * LANES)
        term = dot_nt(g_out[:, span], down_pair(w, pair, 0, width))
        total = term if pair == 0 else total + term
    do_ref[...] = total.astype(BF)
    same = seg_q[...] == seg_k[...]
    for h in range(width // HD):
        cols = slice(h * HD, (h + 1) * HD)
        vcols = slice(width + h * HD, width + (h + 1) * HD)
        s = dot_nt(q_ref[:, cols], kv[:, cols]) * scale
        s = jnp.where(same, s, SCORE_FLOOR)
        prob = jnp.exp(s - lse[:, h : h + 1])
        dp = dot_nt(do_ref[:, cols], kv[:, vcols])
        row = jnp.sum(dp * prob, axis=-1, keepdims=True)
        ds = (prob * (dp - row)).astype(BF)
        dq_out[:, cols] = (dot(ds, kv[:, cols]) * scale).astype(BF)
        grads[:, cols] = dot_tn(ds, q_ref[:, cols]) * scale
        grads[:, vcols] = dot_tn(prob.astype(BF), do_ref[:, cols])
    step = q_ref.shape[0]
    for j in range(m // 2):
        near_out[j] = grads[2 * j * step : (2 * j + 1) * step, :]
        far_out[j] = grads[(2 * j + 1) * step : (2 * j + 2) * step, :].astype(BF)


def qkv_back_body(n, near, got, last, dq, w, kv_out, *pieces):
    width = dq.shape[1]
    halves = width // LANES
    kv_out[...] = (near[0] + got[0].astype(F32) + last[...].astype(F32)).astype(BF)
    total = dot_nt(dq[...], in_matrix(w, 0, halves))
    total = total + dot_nt(kv_out[:, :width], in_matrix(w, 1, halves))
    total = total + dot_nt(kv_out[:, width:], in_matrix(w, 2, halves))
    split_rows(total, pieces)


def attn_grad_body(x_ref, dq, dkv, o_ref, g_ref, out, sums):
    x = x_ref[...]
    width = dq.shape[1]
    halves = width // LANES
    blocks = out.shape[0]
    for c in range(3):
        d = dq[...] if c == 0 else dkv[:, (c - 1) * width : c * width]
        grad = dot_tn(x, d).astype(BF).reshape(blocks, LANES, width)
        for h in range(halves):
            first = (c * halves + h) * LANES
            out[:, first : first + LANES, :] = grad[:, :, h * LANES : (h + 1) * LANES]
    first = 3 * width
    o = o_ref[...]
    for pair in range(blocks // 2):
        span = slice(2 * pair * LANES, (2 * pair + 2) * LANES)
        grad = dot_tn(o, g_ref[:, span]).astype(BF)
        for j in range(2):
            out[2 * pair + j, first : first + width, :] = grad[:, j * LANES : (j + 1) * LANES]
    sums[...] = jnp.zeros_like(sums)
    sums[0:1, :] = jnp.sum(dq[...].astype(F32), axis=0, keepdims=True)
    sums[1:2, :] = jnp.sum(dkv[:, width:].astype(F32), axis=0, keepdims=True)


def shards(sizes, *args):
    shard_n, ctx_n, tp_n = sizes
    (
        hidden_in,
        seg_ids,
        attn_in,
        attn_bias,
        attn_out,
        ff_in,
        ff_bias,
        ff_out,
        gains,
        shifts,
        cotangent,
    ) = args
    packs, tok, depth = hidden_in.shape
    layers = attn_in.shape[0]
    width = attn_in.shape[3]
    hidden = ff_in.shape[2]
    plane_n = shard_n * ctx_n
    blocks = depth // LANES
    fast = (shard_n, ctx_n) == (2, 4) and blocks == 8
    step = tok // tp_n
    tp_me = lax.axis_index("tp")
    ctx_me = lax.axis_index("ctx")
    me = lax.axis_index("shard") * ctx_n + ctx_me
    share = depth // plane_n

    smalls = jnp.concatenate(
        [
            gains.reshape(2 * layers, share),
            shifts.reshape(4 * layers, share),
            ff_bias.reshape(layers, -1),
            attn_bias.reshape(-1, share),
        ],
        axis=0,
    )
    used = smalls.shape[0]
    smalls = jnp.pad(smalls, ((0, -used % 16), (0, 0)))

    first_in, rows = gather_first(attn_in[0], smalls, shard_n, ctx_n, me, fast)
    rest = [gather_rest(ff_in[l], ff_out[l], attn_out[l], fast) for l in range(layers)]
    stacks = [first_in] + [gather_in(attn_in[l], fast) for l in range(1, layers)]

    rows_f = rows.astype(F32)
    at = 6 * layers
    gain_row = lambda l, j: rows_f[2 * l + j][None]
    shift_row = lambda l, j: rows_f[2 * layers + 4 * l + j][None]
    up_bias = lambda l: rows_f[at + l][None]
    qv_bias = (
        rows_f[at + layers : used]
        .reshape(-1, plane_n, share)
        .transpose(1, 0, 2)
        .reshape(plane_n, layers, 2, width // plane_n)
        .transpose(1, 2, 0, 3)
        .reshape(layers, 2, width)
    )

    x_pieces = reorder(hidden_in.reshape(tp_n, step, depth), tp_me)
    seg_cut = reorder(seg_ids.reshape(ctx_n, tp_n, step), ctx_me)
    seg_cut = reorder(seg_cut.transpose(1, 0, 2), tp_me).transpose(1, 0, 2)
    seg_k = seg_cut.reshape(1, -1)
    seg_q = seg_cut[0].reshape(tok, 1)
    keys = ctx_n * tok
    heads = width // HD

    def piece_shapes():
        return [sds((step, depth), F32)] + [sds((step, depth), BF)] * (tp_n - 1)

    ff_w = [r[:, : 2 * hidden] for r in rest]
    out_w = [r[:, 2 * hidden :] for r in rest]
    matmul = lambda *dims: 2 * functools.reduce(lambda a, b: a * b, dims)

    base = x_pieces[0].astype(F32)
    low = [x_pieces[k] for k in range(tp_n)]
    kept = []
    for l in range(layers):
        x, q, kv = call(
            functools.partial(qkv_body, tp_n),
            [sds((tok, depth), BF), sds((tok, width), BF), sds((tok, 2 * width), BF)],
            [whole()] * (tp_n + 2),
            *low,
            stacks[l],
            qv_bias[l],
            flops=matmul(tok, depth, 3 * width),
            name="project_in",
        )
        over_y = swap(kv, "ctx", ctx_n, 2)
        over_core = swap(kv, "ctx", ctx_n, 1)
        over_both = swap(over_y, "ctx", ctx_n, 1)
        o, lse, kv_all, *a_pieces = call(
            functools.partial(attend_body, ctx_n, tp_n),
            [sds((tok, width), BF), sds((tok, heads), F32), sds((keys, 2 * width), BF)]
            + piece_shapes(),
            [whole()] * (ctx_n + 4),
            q,
            kv,
            over_core,
            over_y,
            over_both,
            seg_q,
            seg_k,
            out_w[l],
            flops=matmul(tok, keys, 2 * width) + matmul(tok, width, depth),
            name="attend",
        )
        got = swap_all(a_pieces, "tp", tp_n)

        def norm(base, own, got, shift, gain, move):
            return call(
                functools.partial(norm_body, tp_n),
                [
                    sds((step, depth), F32),
                    sds((step, depth), BF),
                    sds((step, depth), F32),
                    sds((step, LANES), F32),
                ],
                [whole()] * (tp_n + 4),
                base,
                own,
                *got,
                shift,
                gain,
                move,
                name="norm",
            )

        hid, hid_low, n1, inv1 = norm(
            base, a_pieces[0], got, shift_row(l, 0), gain_row(l, 0), shift_row(l, 1)
        )
        h_got = swap_all([hid_low] * tp_n, "tp", tp_n)
        h, slope, act, *f_pieces = call(
            functools.partial(ff_body, tp_n),
            [sds((tok, depth), BF), sds((tok, hidden), F32), sds((tok, hidden), BF)]
            + piece_shapes(),
            [whole()] * (tp_n + 2),
            hid_low,
            *h_got,
            ff_w[l],
            up_bias(l),
            flops=2 * matmul(tok, depth, hidden),
            name="feed_forward",
        )
        got = swap_all(f_pieces, "tp", tp_n)
        base, y_low, n2, inv2 = norm(
            hid, f_pieces[0], got, shift_row(l, 2), gain_row(l, 1), shift_row(l, 3)
        )
        low = [y_low] + swap_all([y_low] * tp_n, "tp", tp_n)
        kept.append((x, q, kv_all, lse, o, n1, inv1, h, slope, act, n2, inv2))
    hidden_out = reorder(jnp.stack(low), tp_me).reshape(packs, tok, depth)

    def norm_back(base, pieces, normed, inverse, gain):
        return call(
            functools.partial(norm_back_body, len(pieces)),
            [sds((step, depth), F32), sds((step, depth), BF), sds((8, depth), F32)],
            [whole()] * (4 + len(pieces)),
            base,
            *pieces,
            normed,
            inverse,
            gain,
            name="norm_back",
        )

    grad = pick(cotangent.reshape(tp_n, step, depth), tp_me).astype(F32)
    terms = []
    row_sums = [None] * layers
    ff_grads = [None] * layers
    attn_grads = [None] * layers
    for l in reversed(range(layers)):
        x, q, kv_all, lse, o, n1, inv1, h, slope, act, n2, inv2 = kept[l]
        dr2, df_low, sums2 = norm_back(grad, terms, n2, inv2, gain_row(l, 1))
        got = swap_all([df_low] * tp_n, "tp", tp_n)
        df, du, sums_up, *h_pieces = pl.pallas_call(
            functools.partial(ff_back_body, tp_n),
            out_shape=[sds((tok, depth), BF), sds((tok, hidden), BF), sds((8, hidden), F32)]
            + piece_shapes(),
            in_specs=[whole()] * (tp_n + 2),
            out_specs=[whole()] * (3 + tp_n),
            scratch_shapes=[pltpu.VMEM((tok, hidden), F32)],
            compiler_params=pltpu.CompilerParams(vmem_limit_bytes=40 * 1024 * 1024),
            cost_estimate=pl.CostEstimate(
                flops=2 * matmul(tok, depth, hidden),
                bytes_accessed=10 * 1024 * 1024,
                transcendentals=0,
            ),
            name="feed_forward_back",
        )(df_low, *got, ff_w[l], slope)
        got = swap_all(h_pieces, "tp", tp_n)
        (packed,) = call(
            ff_grad_body,
            [sds((blocks, 2 * hidden, LANES), BF)],
            [whole()] * 4,
            h,
            act,
            df,
            du,
            flops=2 * matmul(tok, depth, hidden),
            name="feed_forward_grad",
        )
        ff_grads[l] = scatter_ff(packed, hidden, fast)
        dr1, da_low, sums1 = norm_back(dr2, [h_pieces[0], *got], n1, inv1, gain_row(l, 0))
        got = swap_all([da_low] * tp_n, "tp", tp_n)
        da, dq, near, far = pl.pallas_call(
            functools.partial(attend_back_body, tp_n, ctx_n),
            out_shape=[
                sds((tok, depth), BF),
                sds((tok, width), BF),
                sds((ctx_n // 2, tok, 2 * width), F32),
                sds((ctx_n // 2, tok, 2 * width), BF),
            ],
            in_specs=[whole()] * (tp_n + 6),
            out_specs=[whole()] * 4,
            scratch_shapes=[pltpu.VMEM((tok, width), BF), pltpu.VMEM((keys, 2 * width), F32)],
            compiler_params=pltpu.CompilerParams(vmem_limit_bytes=40 * 1024 * 1024),
            cost_estimate=pl.CostEstimate(
                flops=5 * matmul(tok, keys, width) + matmul(tok, width, depth),
                bytes_accessed=8 * 1024 * 1024,
                transcendentals=0,
            ),
            name="attend_back",
        )(da_low, *got, out_w[l], q, kv_all, lse, seg_q, seg_k)
        got = swap(far, "ctx", ctx_n, 1)
        passed = (near[1] + got[1].astype(F32)).astype(BF)
        last = swap(passed, "ctx", ctx_n, 2)
        dkv, *x_pieces = call(
            functools.partial(qkv_back_body, tp_n),
            [sds((tok, 2 * width), BF)] + piece_shapes(),
            [whole()] * 5,
            near,
            got,
            last,
            dq,
            stacks[l],
            flops=matmul(tok, depth, 3 * width),
            name="project_in_back",
        )
        packed, sums_qv = call(
            attn_grad_body,
            [sds((blocks, 4 * width, LANES), BF), sds((8, width), F32)],
            [whole()] * 5,
            x,
            dq,
            dkv,
            o,
            da,
            flops=matmul(tok, depth, 4 * width),
            name="attend_grad",
        )
        attn_grads[l] = scatter_attn(packed, width, fast)
        grad = dr1
        terms = [x_pieces[0], *swap_all(x_pieces, "tp", tp_n)]
        row_sums[l] = (sums1, sums2, sums_up, sums_qv)

    total = grad + terms[0]
    for term in terms[1:]:
        total = total + term.astype(F32)
    total = total.astype(BF)
    pieces = [total] + swap_all([total] * tp_n, "tp", tp_n)
    grad_in = reorder(jnp.stack(pieces), tp_me).astype(F32).reshape(packs, tok, depth)

    small = []
    for sums1, sums2, _, _ in row_sums:
        small += [sums1[0:1], sums2[0:1]]
    for sums1, sums2, _, _ in row_sums:
        small += [sums1[2:3], sums1[1:2], sums2[2:3], sums2[1:2]]
    for _, _, sums_up, _ in row_sums:
        small += [sums_up[0:1]]
    qv = jnp.stack([s[3][0:2] for s in row_sums])
    qv = qv.reshape(layers, 2, plane_n, width // plane_n).transpose(2, 0, 1, 3)
    lines = jnp.concatenate(small, axis=0).reshape(-1, plane_n, share).transpose(1, 0, 2)
    lines = jnp.concatenate([lines, qv.reshape(plane_n, -1, share)], axis=1)
    lines = lax.all_to_all(lines, PLANE, 0, 0, tiled=True)
    lines = jnp.sum(lines, axis=0)
    norms = lines[: 6 * layers]
    flip = 1
    while flip < tp_n:
        norms = norms + swap(norms, "tp", tp_n, flip)
        flip *= 2
    grad_gains = norms[: 2 * layers].reshape(layers, 2, share)
    grad_shifts = norms[2 * layers :].reshape(layers, 4, share)
    grad_ff_bias = lines[6 * layers : 7 * layers].reshape(ff_bias.shape)
    grad_attn_bias = lines[7 * layers :].reshape(attn_bias.shape)

    return (
        hidden_out,
        grad_in,
        jnp.stack([g[0] for g in attn_grads]),
        grad_attn_bias,
        jnp.stack([g[1] for g in attn_grads]),
        jnp.stack([g[0] for g in ff_grads]),
        grad_ff_bias,
        jnp.stack([g[1] for g in ff_grads]),
        grad_gains,
        grad_shifts,
    )


def solution(mesh):
    in_specs = (
        P("shard", "ctx", None),
        P("shard", None),
        P(None, None, ("shard", "ctx"), "tp"),
        P(None, None, "tp", ("shard", "ctx")),
        P(None, "tp", ("shard", "ctx")),
        P(None, ("shard", "ctx"), "tp"),
        P(None, "tp", ("shard", "ctx")),
        P(None, "tp", ("shard", "ctx")),
        P(None, None, ("shard", "ctx")),
        P(None, None, ("shard", "ctx")),
        P("shard", "ctx", None),
    )
    out_specs = (
        P("shard", "ctx", None),
        P("shard", "ctx", None),
        P(None, None, ("shard", "ctx"), "tp"),
        P(None, None, "tp", ("shard", "ctx")),
        P(None, "tp", ("shard", "ctx")),
        P(None, ("shard", "ctx"), "tp"),
        P(None, "tp", ("shard", "ctx")),
        P(None, "tp", ("shard", "ctx")),
        P(None, None, ("shard", "ctx")),
        P(None, None, ("shard", "ctx")),
    )
    sizes = (mesh.shape["shard"], mesh.shape["ctx"], mesh.shape["tp"])
    return jax.shard_map(
        functools.partial(shards, sizes),
        mesh=mesh,
        in_specs=in_specs,
        out_specs=out_specs,
        check_vma=False,
    )
```

```python
import functools

import jax
import jax.numpy as jnp
from jax import lax
from jax.experimental import pallas as pl
from jax.experimental.pallas import tpu as pltpu
from jax.sharding import PartitionSpec as P

HD = 64
LANES = 128
SCORE_FLOOR = -1e30
PLANE = ("shard", "ctx")
BF = jnp.bfloat16
F32 = jnp.float32
VMEM_GRANT = 16 * 1024 * 1024


def dot(left, right):
    return jnp.dot(left, right, preferred_element_type=F32)


def dot_nt(left, right):
    return lax.dot_general(left, right, (((1,), (1,)), ((), ())), preferred_element_type=F32)


def dot_tn(left, right):
    return lax.dot_general(left, right, (((0,), (0,)), ((), ())), preferred_element_type=F32)


def sds(shape, kind):
    return jax.ShapeDtypeStruct(shape, kind)


def whole():
    return pl.BlockSpec(memory_space=pltpu.VMEM)


def call(body, out_shape, *operands, flops=0, scratch=(), name=None):
    moved = sum(o.size * o.dtype.itemsize for o in operands)
    moved += sum(o.size * o.dtype.itemsize for o in out_shape)
    scalar = pl.BlockSpec(memory_space=pltpu.SMEM)
    return pl.pallas_call(
        body,
        out_shape=out_shape,
        in_specs=[scalar if o.dtype == jnp.int32 and o.ndim == 1 else whole() for o in operands],
        out_specs=[whole() for _ in out_shape],
        scratch_shapes=scratch,
        compiler_params=pltpu.CompilerParams(vmem_limit_bytes=VMEM_GRANT),
        cost_estimate=pl.CostEstimate(flops=flops, bytes_accessed=moved, transcendentals=0),
        name=name,
    )(*operands)


def tie(value, after):
    return lax.optimization_barrier((value, after))[0]


def swap(value, axis, size, flip):
    return lax.ppermute(value, axis, [(i, i ^ flip) for i in range(size)])


def swap_all(pieces, axis, size):
    order = [k for k in (2, 3, 1) if k < size] + list(range(4, size))
    got = {k: swap(pieces[k], axis, size, k) for k in order}
    return [got[k] for k in range(1, size)]


def pick(blocks, index):
    return lax.dynamic_index_in_dim(blocks, index, 0, False)


def reorder(blocks, me):
    return jnp.stack([pick(blocks, me ^ k) for k in range(blocks.shape[0])])


def pack_in(matrix):
    c, rows, cols = matrix.shape
    return matrix.reshape(c, rows, cols // LANES, LANES).transpose(0, 2, 1, 3).reshape(-1, LANES)


def unpack_in(packed, c, rows, cols):
    return (
        packed.reshape(c, cols // LANES, rows, LANES).transpose(0, 2, 1, 3).reshape(c, rows, cols)
    )


def blocks_of_rows(matrix):
    c, depth, cols = matrix.shape
    cut = matrix.reshape(c, depth // LANES, LANES, cols // LANES, LANES)
    return cut.transpose(1, 0, 3, 2, 4).reshape(depth // LANES, -1, LANES)


def rows_of_blocks(packed, c, cols):
    blocks = packed.shape[0]
    cut = packed.reshape(blocks, c, cols // LANES, LANES, LANES)
    return cut.transpose(1, 0, 3, 2, 4).reshape(c, blocks * LANES, cols)


def blocks_of_cols(matrix):
    rows, width = matrix.shape
    return matrix.reshape(rows, width // LANES, LANES).transpose(1, 0, 2)


def cols_of_blocks(packed):
    blocks, rows, _ = packed.shape
    return packed.transpose(1, 0, 2).reshape(rows, blocks * LANES)


def gather_first(attn_in, attn_out, small, me, fast):
    if not fast:
        gains, shifts, ff_bias, attn_bias = small
        layers, _, share = gains.shape
        rows = jnp.concatenate(
            [
                gains.reshape(2 * layers, share),
                shifts.reshape(4 * layers, share),
                ff_bias.reshape(layers, -1),
            ],
            axis=0,
        )
        rows = lax.all_gather(rows, PLANE, axis=1, tiled=True)
        bias = lax.all_gather(attn_bias, PLANE, axis=3, tiled=True)
        return gather_attn(attn_in, attn_out, 0, fast), rows, bias.reshape(layers, 2, -1)
    layers = attn_in.shape[0]
    count = 3 * attn_in.shape[3] + attn_out.shape[1] + 32
    (own,) = call(
        pack_first_body,
        [sds((count, LANES), BF)],
        attn_in,
        attn_out,
        *small,
        scratch=[pltpu.VMEM((32, LANES), F32)],
        name="pack_first",
    )
    half = count // 2
    over_x = swap(own, "shard", 2, 1)
    over_y = swap(own, "ctx", 4, 2)
    first = swap(over_y[:half], "shard", 2, 1)
    second = swap(over_x[half:], "ctx", 4, 2)
    near = [own, over_y, over_x, first, second]
    far = [swap(piece, "ctx", 4, 1) for piece in near]
    (natural,) = call(
        assemble_body, [sds((8, count, LANES), BF)], me.reshape(1), *near, *far, name="assemble"
    )
    small_rows = natural[:, -32:].transpose(1, 0, 2)
    used = 7 * layers
    rows = small_rows[:used].reshape(used, -1)
    bias = small_rows[used : used + 2 * layers, :, : small[3].shape[3]]
    return natural, rows, bias.reshape(layers, 2, -1)


def gather_attn(attn_in, attn_out, layer, fast):
    if not fast:
        full = lax.all_gather(attn_in[layer], PLANE, axis=1, tiled=True)
        out = lax.all_gather(attn_out[layer], PLANE, axis=1, tiled=True)
        return jnp.concatenate([blocks_of_rows(full), blocks_of_cols(out)], axis=1)
    count = 3 * attn_in.shape[3] + attn_out.shape[1]
    (own,) = call(
        functools.partial(pack_attn_body, layer),
        [sds((count, LANES), BF)],
        attn_in,
        attn_out,
        name="pack_attention",
    )
    return lax.all_gather(own, PLANE, axis=0, tiled=False)


def gather_ff(ff_in, ff_out, layer, fast):
    if not fast:
        up = lax.all_gather(ff_in[layer], PLANE, axis=0, tiled=True)
        down = lax.all_gather(ff_out[layer], PLANE, axis=1, tiled=True)
        return jnp.concatenate([blocks_of_rows(up[None]), blocks_of_cols(down)], axis=1)
    (own,) = call(
        functools.partial(pack_ff_body, layer),
        [sds((2 * ff_in.shape[2], LANES), BF)],
        ff_in,
        ff_out,
        name="pack_feed_forward",
    )
    return lax.all_gather(own, PLANE, axis=0, tiled=False)


def scatter_natural(packed, fast):
    return lax.psum_scatter(packed, PLANE, scatter_dimension=0, tiled=False).astype(F32)


def scatter_permute(near, far):
    _, count, _ = near.shape
    half = count // 2
    rest = count - half
    got = swap(far, "ctx", 4, 1)
    keep_a, send_a, keep_b, send_b = call(
        reduce_core_body,
        [
            sds((2, half, LANES), F32),
            sds((2, half, LANES), BF),
            sds((2, rest, LANES), F32),
            sds((2, rest, LANES), BF),
        ],
        near,
        got,
        name="reduce_core",
    )
    got_a = swap(send_a, "shard", 2, 1)
    got_b = swap(send_b, "ctx", 4, 2)
    keep_a, send_a, keep_b, send_b = call(
        reduce_plane_body,
        [
            sds((half, LANES), F32),
            sds((half, LANES), BF),
            sds((rest, LANES), F32),
            sds((rest, LANES), BF),
        ],
        keep_a,
        got_a,
        keep_b,
        got_b,
        name="reduce_plane",
    )
    got_a = swap(send_a, "ctx", 4, 2)
    got_b = swap(send_b, "shard", 2, 1)
    (own,) = call(
        reduce_last_body,
        [sds((count, LANES), F32)],
        keep_a,
        got_a,
        keep_b,
        got_b,
        name="reduce_last",
    )
    return own


def cut_ff(own, hidden):
    return unpack_in(own[:hidden], 1, LANES, hidden)[0], own[hidden:]


def cut_attn(own, width):
    cut = 3 * width
    return unpack_in(own[:cut], 3, LANES, width), own[cut : cut + width]


def scatter_whole_ff(packed, hidden):
    up = rows_of_blocks(packed[:, :hidden], 1, hidden)[0]
    down = cols_of_blocks(packed[:, hidden:])
    return (
        lax.psum_scatter(up, PLANE, scatter_dimension=0, tiled=True).astype(F32),
        lax.psum_scatter(down, PLANE, scatter_dimension=1, tiled=True).astype(F32),
    )


def scatter_whole_attn(packed, width):
    cut = 3 * width
    stack = rows_of_blocks(packed[:, :cut], 3, width)
    out = cols_of_blocks(packed[:, cut : cut + width])
    return (
        lax.psum_scatter(stack, PLANE, scatter_dimension=1, tiled=True).astype(F32),
        lax.psum_scatter(out, PLANE, scatter_dimension=1, tiled=True).astype(F32),
    )


def join(refs, target):
    step = refs[0].shape[0]
    for k, ref in enumerate(refs):
        target[k * step : (k + 1) * step, :] = ref[...]


def split_rows(value, refs, columns=slice(None)):
    step = refs[0].shape[0]
    for k, ref in enumerate(refs):
        ref[:, columns] = value[k * step : (k + 1) * step].astype(ref.dtype)


def in_matrix(w, c, halves):
    depth = w.shape[0] * LANES
    return jnp.concatenate(
        [
            w[:, (c * halves + h) * LANES : (c * halves + h + 1) * LANES, :].reshape(depth, LANES)
            for h in range(halves)
        ],
        axis=1,
    )


def up_pair(w, pair):
    depth = w.shape[0] * LANES
    return jnp.concatenate(
        [w[:, n * LANES : (n + 1) * LANES, :].reshape(depth, LANES) for n in (2 * pair, 2 * pair + 1)],
        axis=1,
    )


def down_pair(w, pair, first, count):
    return jnp.concatenate(
        [w[s, first : first + count, :] for s in (2 * pair, 2 * pair + 1)], axis=1
    )


def pack_attn_body(layer, attn_in, attn_out, out):
    _, _, depth, width = attn_in.shape
    halves = width // LANES
    for c in range(3):
        for h in range(halves):
            first = (c * halves + h) * depth
            out[first : first + depth, :] = attn_in[layer, c, :, h * LANES : (h + 1) * LANES]
    first = 3 * halves * depth
    out[first : first + attn_out.shape[1], :] = attn_out[layer]


def pack_first_body(attn_in, attn_out, gains, shifts, ff_bias, attn_bias, out, rows):
    pack_attn_body(0, attn_in, attn_out, out)
    layers = gains.shape[0]
    rows[...] = jnp.zeros_like(rows)
    for l in range(layers):
        rows[2 * l : 2 * l + 2, :] = gains[l].astype(F32)
        first = 2 * layers + 4 * l
        rows[first : first + 4, :] = shifts[l].astype(F32)
        first = 6 * layers + l
        rows[first : first + 1, :] = ff_bias[l].astype(F32)
        for c in range(2):
            first = 7 * layers + 2 * l + c
            rows[first : first + 1, : attn_bias.shape[3]] = attn_bias[l, c].astype(F32)
    out[out.shape[0] - 32 :, :] = rows[...].astype(BF)


def pack_ff_body(layer, ff_in, ff_out, out):
    depth, hidden = ff_in.shape[1:]
    for n in range(hidden // LANES):
        out[n * depth : (n + 1) * depth, :] = ff_in[layer, :, n * LANES : (n + 1) * LANES]
    out[hidden : 2 * hidden, :] = ff_out[layer]


def assemble_body(me, *refs):
    near, far, out = refs[:5], refs[5:10], refs[10]
    half = near[3].shape[0]
    for flip, pieces in ((0, near), (1, far)):
        for j in range(3):
            out[me[0] ^ (2 * j + flip)] = pieces[j][...]
        out[me[0] ^ (6 + flip), :half, :] = pieces[3][...]
        out[me[0] ^ (6 + flip), half:, :] = pieces[4][...]


def reduce_core_body(near, got, keep_a, send_a, keep_b, send_b):
    half = keep_a.shape[1]
    for j in range(4):
        head = near[j, :half, :].astype(F32) + got[j, :half, :].astype(F32)
        tail = near[j, half:, :].astype(F32) + got[j, half:, :].astype(F32)
        if j < 2:
            keep_a[j] = head
        else:
            send_a[j - 2] = head.astype(BF)
        if j % 2 == 0:
            keep_b[j // 2] = tail
        else:
            send_b[j // 2] = tail.astype(BF)


def reduce_plane_body(near_a, got_a, near_b, got_b, keep_a, send_a, keep_b, send_b):
    for near, got, keep, send in (
        (near_a, got_a, keep_a, send_a),
        (near_b, got_b, keep_b, send_b),
    ):
        keep[...] = near[0] + got[0].astype(F32)
        send[...] = (near[1] + got[1].astype(F32)).astype(BF)


def reduce_last_body(keep_a, got_a, keep_b, got_b, out):
    half = keep_a.shape[0]
    out[:half, :] = keep_a[...] + got_a[...].astype(F32)
    out[half:, :] = keep_b[...] + got_b[...].astype(F32)


def put(outs, me, pair, rows, even, odd):
    if me is None:
        outs[0][2 * pair, rows, :] = even
        outs[0][2 * pair + 1, rows, :] = odd
        return
    near, far = outs
    slot = pair ^ (me[0] // 2)
    turned = me[0] % 2 == 1
    near[slot, rows, :] = jnp.where(turned, odd, even)
    far[slot, rows, :] = jnp.where(turned, even, odd)


def qkv_body(n, *refs):
    x_refs, (w, bias, x_out, q_out, kv_out) = refs[:n], refs[n:]
    join(x_refs, x_out)
    x = x_out[...]
    width = q_out.shape[1]
    halves = width // LANES
    q_out[...] = (dot(x, in_matrix(w, 0, halves)) + bias[0:1, :]).astype(BF)
    kv_out[:, :width] = dot(x, in_matrix(w, 1, halves)).astype(BF)
    kv_out[:, width:] = (dot(x, in_matrix(w, 2, halves)) + bias[1:2, :]).astype(BF)


def attend_body(m, n, *refs):
    q_ref, kv_refs = refs[0], refs[1 : 1 + m]
    seg_q, seg_k, w = refs[1 + m : 4 + m]
    o_out, lse_out, kv_all = refs[4 + m : 7 + m]
    pieces = refs[7 + m :]
    join(kv_refs, kv_all)
    width = q_ref.shape[1]
    same = seg_q[...] == seg_k[...]
    for h in range(width // HD):
        cols = slice(h * HD, (h + 1) * HD)
        vcols = slice(width + h * HD, width + (h + 1) * HD)
        s = dot_nt(q_ref[:, cols], kv_all[:, cols]) * HD ** (-0.5)
        s = jnp.where(same, s, SCORE_FLOOR)
        top = jnp.max(s, axis=-1, keepdims=True)
        e = jnp.exp(s - top)
        total = jnp.sum(e, axis=-1, keepdims=True)
        prob = (e / total).astype(BF)
        lse_out[:, h : h + 1] = top + jnp.log(total)
        o_out[:, cols] = dot(prob, kv_all[:, vcols]).astype(BF)
    o = o_out[...]
    for pair in range(w.shape[0] // 2):
        span = slice(2 * pair * LANES, (2 * pair + 2) * LANES)
        split_rows(dot(o, down_pair(w, pair, 3 * width, width)), pieces, span)


def norm_body(n, *refs):
    base, own = refs[0], refs[1]
    others = refs[2 : 1 + n]
    shift, gain, centre_shift, out, out_low, normed, inverse = refs[1 + n :]
    r = base[...] + own[...]
    for other in others:
        r = r + other[...].astype(F32)
    r = r + shift[...]
    centre = r - jnp.mean(r, axis=-1, keepdims=True)
    inv = lax.rsqrt(jnp.mean(centre * centre, axis=-1, keepdims=True) + 1e-12)
    norm = centre * inv
    y = norm * gain[...] + centre_shift[...]
    out[...] = y
    out_low[...] = y.astype(BF)
    normed[...] = norm
    inverse[...] = jnp.broadcast_to(inv, inverse.shape)


def ff_body(n, *refs):
    h_refs = refs[:n]
    w, bias, h_out, slope_out, act_out = refs[n : n + 5]
    pieces = refs[n + 5 :]
    join(h_refs, h_out)
    h = h_out[...]
    hidden = act_out.shape[1]
    for pair in range(hidden // (2 * LANES)):
        span = slice(2 * pair * LANES, (2 * pair + 2) * LANES)
        u = dot(h, up_pair(w, pair)) + bias[:, span]
        cdf = 0.5 * (1.0 + lax.erf(u * (0.5**0.5)))
        act_out[:, span] = (u * cdf).astype(BF)
        slope_out[:, span] = cdf + u * (jnp.exp(-0.5 * u * u) * 0.3989422804014327)
    act = act_out[...]
    for pair in range(w.shape[0] // 2):
        span = slice(2 * pair * LANES, (2 * pair + 2) * LANES)
        split_rows(dot(act, down_pair(w, pair, hidden, hidden)), pieces, span)


def norm_back_body(n, *refs):
    base, own = refs[0], refs[1 : 2 if n else 1]
    others = refs[2 : 1 + n] if n else ()
    normed, inverse, gain, grad, grad_low, sums = refs[1 + n :]
    dy = base[...]
    for ref in own:
        dy = dy + ref[...]
    for ref in others:
        dy = dy + ref[...].astype(F32)
    norm = normed[...]
    e = dy * gain[...]
    dr = inverse[:, 0:1] * (
        e
        - jnp.mean(e, axis=-1, keepdims=True)
        - norm * jnp.mean(e * norm, axis=-1, keepdims=True)
    )
    grad[...] = dr
    grad_low[...] = dr.astype(BF)
    sums[...] = jnp.zeros_like(sums)
    sums[0:1, :] = jnp.sum(dy * norm, axis=0, keepdims=True)
    sums[1:2, :] = jnp.sum(dy, axis=0, keepdims=True)
    sums[2:3, :] = jnp.sum(dr, axis=0, keepdims=True)


def ff_back_body(n, *refs):
    g_refs = refs[:n]
    w, slope, g_out, du_out, bias_out = refs[n : n + 5]
    pieces = refs[n + 5 : 2 * n + 5]
    total = refs[2 * n + 5]
    join(g_refs, g_out)
    hidden = du_out.shape[1]
    for pair in range(w.shape[0] // 2):
        span = slice(2 * pair * LANES, (2 * pair + 2) * LANES)
        term = dot_nt(g_out[:, span], down_pair(w, pair, hidden, hidden))
        total[...] = term if pair == 0 else total[...] + term
    du = (total[...] * slope[...]).astype(BF)
    du_out[...] = du
    bias_out[...] = jnp.broadcast_to(
        jnp.sum(du.astype(F32), axis=0, keepdims=True), bias_out.shape
    )
    for pair in range(hidden // (2 * LANES)):
        span = slice(2 * pair * LANES, (2 * pair + 2) * LANES)
        term = dot_nt(du_out[:, span], up_pair(w, pair))
        total[...] = term if pair == 0 else total[...] + term
    split_rows(total[...], pieces)


def ff_grad_body(turn, *refs):
    me = refs[0] if turn else None
    h_ref, act_ref, g_ref, du_ref = refs[turn : turn + 4]
    outs = refs[turn + 4 :]
    h, act = h_ref[...], act_ref[...]
    hidden = act.shape[1]
    blocks = g_ref.shape[1] // LANES
    for pair in range(hidden // (2 * LANES)):
        span = slice(2 * pair * LANES, (2 * pair + 2) * LANES)
        grad = dot_tn(h, du_ref[:, span]).astype(BF)
        for j in range(2):
            rows = slice((2 * pair + j) * LANES, (2 * pair + j + 1) * LANES)
            cols = slice(j * LANES, (j + 1) * LANES)
            for q in range(blocks // 2):
                first = 2 * q * LANES
                put(
                    outs,
                    me,
                    q,
                    rows,
                    grad[first : first + LANES, cols],
                    grad[first + LANES : first + 2 * LANES, cols],
                )
    for pair in range(blocks // 2):
        span = slice(2 * pair * LANES, (2 * pair + 2) * LANES)
        grad = dot_tn(act, g_ref[:, span]).astype(BF)
        put(outs, me, pair, slice(hidden, 2 * hidden), grad[:, :LANES], grad[:, LANES:])


def attend_back_body(n, m, *refs):
    g_refs = refs[:n]
    w, q_ref, kv, lse, seg_q, seg_k, g_out, dq_out, near_out, far_out, do_ref, grads = refs[n:]
    join(g_refs, g_out)
    width = q_ref.shape[1]
    scale = HD ** (-0.5)
    for pair in range(w.shape[0] // 2):
        span = slice(2 * pair * LANES, (2 * pair + 2) * LANES)
        term = dot_nt(g_out[:, span], down_pair(w, pair, 3 * width, width))
        total = term if pair == 0 else total + term
    do_ref[...] = total.astype(BF)
    same = seg_q[...] == seg_k[...]
    for h in range(width // HD):
        cols = slice(h * HD, (h + 1) * HD)
        vcols = slice(width + h * HD, width + (h + 1) * HD)
        s = dot_nt(q_ref[:, cols], kv[:, cols]) * scale
        s = jnp.where(same, s, SCORE_FLOOR)
        prob = jnp.exp(s - lse[:, h : h + 1])
        dp = dot_nt(do_ref[:, cols], kv[:, vcols])
        row = jnp.sum(dp * prob, axis=-1, keepdims=True)
        ds = (prob * (dp - row)).astype(BF)
        dq_out[:, cols] = (dot(ds, kv[:, cols]) * scale).astype(BF)
        grads[:, cols] = dot_tn(ds, q_ref[:, cols]) * scale
        grads[:, vcols] = dot_tn(prob.astype(BF), do_ref[:, cols])
    step = q_ref.shape[0]
    for j in range(m // 2):
        near_out[j] = grads[2 * j * step : (2 * j + 1) * step, :]
        far_out[j] = grads[(2 * j + 1) * step : (2 * j + 2) * step, :].astype(BF)


def qkv_back_body(n, near, got, last, dq, w, kv_out, *pieces):
    width = dq.shape[1]
    halves = width // LANES
    kv_out[...] = (near[0] + got[0].astype(F32) + last[...].astype(F32)).astype(BF)
    total = dot_nt(dq[...], in_matrix(w, 0, halves))
    total = total + dot_nt(kv_out[:, :width], in_matrix(w, 1, halves))
    total = total + dot_nt(kv_out[:, width:], in_matrix(w, 2, halves))
    split_rows(total, pieces)


def attn_grad_body(turn, *refs):
    me = refs[0] if turn else None
    x_ref, dq, dkv, o_ref, g_ref = refs[turn : turn + 5]
    lines, biases = refs[turn + 5 : turn + 7] if turn else (None, None)
    outs, sums = refs[5 + 3 * turn : -1], refs[-1]
    x = x_ref[...]
    width = dq.shape[1]
    halves = width // LANES
    blocks = g_ref.shape[1] // LANES
    for c in range(3):
        d = dq[...] if c == 0 else dkv[:, (c - 1) * width : c * width]
        grad = dot_tn(x, d).astype(BF)
        for h in range(halves):
            rows = slice((c * halves + h) * LANES, (c * halves + h + 1) * LANES)
            cols = slice(h * LANES, (h + 1) * LANES)
            for q in range(blocks // 2):
                first = 2 * q * LANES
                put(
                    outs,
                    me,
                    q,
                    rows,
                    grad[first : first + LANES, cols],
                    grad[first + LANES : first + 2 * LANES, cols],
                )
    o = o_ref[...]
    for pair in range(blocks // 2):
        span = slice(2 * pair * LANES, (2 * pair + 2) * LANES)
        grad = dot_tn(o, g_ref[:, span]).astype(BF)
        put(outs, me, pair, slice(3 * width, 4 * width), grad[:, :LANES], grad[:, LANES:])
    sums[...] = jnp.zeros_like(sums)
    sums[0:1, :] = jnp.sum(dq[...].astype(F32), axis=0, keepdims=True)
    sums[1:2, :] = jnp.sum(dkv[:, width:].astype(F32), axis=0, keepdims=True)
    if turn:
        count = lines.shape[0]
        both = jnp.concatenate([sums[...], biases[...]], axis=0).astype(BF)
        low = lines[...].astype(BF)
        per = blocks // halves
        for pair in range(blocks // 2):
            cut = [
                jnp.concatenate(
                    [
                        low[:, s * LANES : (s + 1) * LANES],
                        both[:, s // per * LANES : (s // per + 1) * LANES],
                    ],
                    axis=0,
                )
                for s in (2 * pair, 2 * pair + 1)
            ]
            put(outs, me, pair, slice(4 * width, 4 * width + count + 16), *cut)


def shards(sizes, *args):
    shard_n, ctx_n, tp_n = sizes
    (
        hidden_in,
        seg_ids,
        attn_in,
        attn_bias,
        attn_out,
        ff_in,
        ff_bias,
        ff_out,
        gains,
        shifts,
        cotangent,
    ) = args
    packs, tok, depth = hidden_in.shape
    layers = attn_in.shape[0]
    width = attn_in.shape[3]
    hidden = ff_in.shape[2]
    plane_n = shard_n * ctx_n
    blocks = depth // LANES
    fast = (shard_n, ctx_n, blocks, layers) == (2, 4, 8, 2)
    step = tok // tp_n
    share = depth // plane_n
    keys = ctx_n * tok
    heads = width // HD
    tp_me = lax.axis_index("tp")
    ctx_me = lax.axis_index("ctx")
    me = (lax.axis_index("shard") * ctx_n + ctx_me).astype(jnp.int32)

    first, rows, qv_bias = gather_first(
        attn_in, attn_out, (gains, shifts, ff_bias, attn_bias), me, fast
    )
    ff_w = [None] * layers
    attn_w = [first] + [None] * (layers - 1)
    for l in range(layers):
        if l > 0:
            attn_w[l] = gather_attn(attn_in, attn_out, l, fast)
        ff_w[l] = gather_ff(ff_in, ff_out, l, fast)

    rows_f = rows.astype(F32)
    qv_bias = qv_bias.astype(F32)
    gain_row = lambda l, j: rows_f[2 * l + j][None]
    shift_row = lambda l, j: rows_f[2 * layers + 4 * l + j][None]
    up_bias = lambda l: rows_f[6 * layers + l][None]

    x_pieces = reorder(hidden_in.reshape(tp_n, step, depth), tp_me)
    seg_cut = reorder(seg_ids.reshape(ctx_n, tp_n, step), ctx_me)
    seg_cut = reorder(seg_cut.transpose(1, 0, 2), tp_me).transpose(1, 0, 2)
    seg_k = seg_cut.reshape(1, -1)
    seg_q = seg_cut[0].reshape(tok, 1)

    def piece_shapes():
        return [sds((step, depth), F32)] + [sds((step, depth), BF)] * (tp_n - 1)

    def matmul(*dims):
        return 2 * functools.reduce(lambda a, b: a * b, dims)

    def spread(piece):
        return [piece] + swap_all([piece] * tp_n, "tp", tp_n)

    def norm(base, own, got, shift, gain, move):
        return call(
            functools.partial(norm_body, tp_n),
            [
                sds((step, depth), F32),
                sds((step, depth), BF),
                sds((step, depth), F32),
                sds((step, LANES), F32),
            ],
            base,
            own,
            *got,
            shift,
            gain,
            move,
            name="norm",
        )

    def norm_back(base, pieces, normed, inverse, gain):
        return call(
            functools.partial(norm_back_body, len(pieces)),
            [sds((step, depth), F32), sds((step, depth), BF), sds((8, depth), F32)],
            base,
            *pieces,
            normed,
            inverse,
            gain,
            name="norm_back",
        )

    base = x_pieces[0].astype(F32)
    low = [x_pieces[k] for k in range(tp_n)]
    kept = []
    for l in range(layers):
        x, q, kv = call(
            functools.partial(qkv_body, tp_n),
            [sds((tok, depth), BF), sds((tok, width), BF), sds((tok, 2 * width), BF)],
            *low,
            attn_w[l],
            qv_bias[l],
            flops=matmul(tok, depth, 3 * width),
            name="project_in",
        )
        over_y = swap(kv, "ctx", ctx_n, 2)
        over_core = swap(kv, "ctx", ctx_n, 1)
        over_both = swap(over_y, "ctx", ctx_n, 1)
        o, lse, kv_all, *a_pieces = call(
            functools.partial(attend_body, ctx_n, tp_n),
            [sds((tok, width), BF), sds((tok, heads), F32), sds((keys, 2 * width), BF)]
            + piece_shapes(),
            q,
            kv,
            over_core,
            over_y,
            over_both,
            seg_q,
            seg_k,
            attn_w[l],
            flops=matmul(tok, keys, 2 * width) + matmul(tok, width, depth),
            name="attend",
        )
        got = swap_all(a_pieces, "tp", tp_n)
        hid, hid_low, n1, inv1 = norm(
            base, a_pieces[0], got, shift_row(l, 0), gain_row(l, 0), shift_row(l, 1)
        )
        h, slope, act, *f_pieces = call(
            functools.partial(ff_body, tp_n),
            [sds((tok, depth), BF), sds((tok, hidden), F32), sds((tok, hidden), BF)]
            + piece_shapes(),
            *spread(hid_low),
            ff_w[l],
            up_bias(l),
            flops=2 * matmul(tok, depth, hidden),
            name="feed_forward",
        )
        got = swap_all(f_pieces, "tp", tp_n)
        base, y_low, n2, inv2 = norm(
            hid, f_pieces[0], got, shift_row(l, 2), gain_row(l, 1), shift_row(l, 3)
        )
        if l < layers - 1:
            low = spread(y_low)
        kept.append((x, q, kv_all, lse, o, n1, inv1, h, slope, act, n2, inv2))

    grad = pick(cotangent.reshape(tp_n, step, depth), tp_me).astype(F32)
    terms = []
    row_sums = [None] * layers
    qv_sums = [None] * layers
    ff_grads = [None] * layers
    attn_grads = [None] * layers
    lines = []
    for l in reversed(range(layers)):
        turn = int(fast and l == 0)
        where = [me.reshape(1)] * turn
        x, q, kv_all, lse, o, n1, inv1, h, slope, act, n2, inv2 = kept[l]
        dr2, df_low, sums2 = norm_back(grad, terms, n2, inv2, gain_row(l, 1))
        df, du, sums_up, *h_pieces = call(
            functools.partial(ff_back_body, tp_n),
            [sds((tok, depth), BF), sds((tok, hidden), BF), sds((8, hidden), F32)]
            + piece_shapes(),
            *spread(df_low),
            ff_w[l],
            slope,
            flops=2 * matmul(tok, depth, hidden),
            scratch=[pltpu.VMEM((tok, hidden), F32)],
            name="feed_forward_back",
        )
        got = swap_all(h_pieces, "tp", tp_n)
        packed = call(
            functools.partial(ff_grad_body, turn),
            [sds((blocks // (1 + turn), 2 * hidden, LANES), BF)] * (1 + turn),
            *where,
            h,
            act,
            df,
            du,
            flops=2 * matmul(tok, depth, hidden),
            name="feed_forward_grad",
        )
        got = tie(got, packed)
        if turn:
            ff_grads[l] = cut_ff(scatter_permute(*packed), hidden)
        elif fast:
            ff_grads[l] = cut_ff(scatter_natural(packed[0], fast), hidden)
        else:
            ff_grads[l] = scatter_whole_ff(packed[0], hidden)
        dr1, da_low, sums1 = norm_back(dr2, [h_pieces[0], *got], n1, inv1, gain_row(l, 0))
        row_sums[l] = (sums1, sums2, sums_up)
        da, dq, near, far = call(
            functools.partial(attend_back_body, tp_n, ctx_n),
            [
                sds((tok, depth), BF),
                sds((tok, width), BF),
                sds((ctx_n // 2, tok, 2 * width), F32),
                sds((ctx_n // 2, tok, 2 * width), BF),
            ],
            *spread(da_low),
            attn_w[l],
            q,
            kv_all,
            lse,
            seg_q,
            seg_k,
            flops=5 * matmul(tok, keys, width) + matmul(tok, width, depth),
            scratch=[pltpu.VMEM((tok, width), BF), pltpu.VMEM((keys, 2 * width), F32)],
            name="attend_back",
        )
        got = swap(far, "ctx", ctx_n, 1)
        if l == layers - 1:
            low = spread(tie(y_low, far))
        if l == 0:
            norms = [s for sums1, sums2, _ in row_sums for s in (sums1[0:1], sums2[0:1])]
            for sums1, sums2, _ in row_sums:
                norms += [sums1[2:3], sums1[1:2], sums2[2:3], sums2[1:2]]
            norms = jnp.concatenate(norms, axis=0)
            flip = 1
            while flip < tp_n:
                norms = norms + swap(norms, "tp", tp_n, flip)
                flip *= 2
            lines = jnp.concatenate([norms] + [s[0:1] for _, _, s in row_sums], axis=0)
            lines = jnp.pad(lines, ((0, -lines.shape[0] % 16), (0, 0)))
        passed = (near[1] + got[1].astype(F32)).astype(BF)
        last = swap(passed, "ctx", ctx_n, 2)
        dkv, *x_pieces = call(
            functools.partial(qkv_back_body, tp_n),
            [sds((tok, 2 * width), BF)] + piece_shapes(),
            near,
            got,
            last,
            dq,
            attn_w[l],
            flops=matmul(tok, depth, 3 * width),
            name="project_in_back",
        )
        got = swap_all(x_pieces, "tp", tp_n)
        count = 4 * width + turn * (lines.shape[0] + 16 if turn else 0)
        *packed, qv_sums[l] = call(
            functools.partial(attn_grad_body, turn),
            [sds((blocks // (1 + turn), count, LANES), BF)] * (1 + turn) + [sds((8, width), F32)],
            *where,
            x,
            dq,
            dkv,
            o,
            da,
            *([lines, qv_sums[1]] if turn else []),
            flops=matmul(tok, depth, 4 * width),
            name="attend_grad",
        )
        got = tie(got, packed)
        if turn:
            own = scatter_permute(*packed)
            attn_grads[l] = cut_attn(own, width)
        elif fast:
            attn_grads[l] = cut_attn(scatter_natural(packed[0], fast), width)
        else:
            attn_grads[l] = scatter_whole_attn(packed[0], width)
        grad = dr1
        terms = [x_pieces[0], *got]

    hidden_out = reorder(jnp.stack(low), tp_me).reshape(packs, tok, depth)
    total = grad + terms[0]
    for term in terms[1:]:
        total = total + term.astype(F32)
    pieces = spread(total.astype(BF))
    grad_in = reorder(jnp.stack(pieces), tp_me).astype(F32).reshape(packs, tok, depth)

    count = lines.shape[0]
    if fast:
        lines = own[4 * width : 4 * width + count]
        narrow = width // plane_n
        bias = own[4 * width + count :].reshape(layers, 8, LANES)[:, :2]
        first = lax.rem(me, LANES // narrow) * narrow
        bias = lax.dynamic_slice_in_dim(bias, first, narrow, 2)
    else:
        lines = lax.psum_scatter(lines, PLANE, scatter_dimension=1, tiled=True)
        bias = jnp.stack([s[0:2] for s in qv_sums])
        bias = lax.psum_scatter(bias, PLANE, scatter_dimension=2, tiled=True)

    return (
        hidden_out,
        grad_in,
        jnp.stack([g[0] for g in attn_grads]),
        bias.reshape(attn_bias.shape),
        jnp.stack([g[1] for g in attn_grads]),
        jnp.stack([g[0] for g in ff_grads]),
        lines[6 * layers : 7 * layers].reshape(ff_bias.shape),
        jnp.stack([g[1] for g in ff_grads]),
        lines[: 2 * layers].reshape(gains.shape),
        lines[2 * layers : 6 * layers].reshape(shifts.shape),
    )


def solution(mesh):
    in_specs = (
        P("shard", "ctx", None),
        P("shard", None),
        P(None, None, ("shard", "ctx"), "tp"),
        P(None, None, "tp", ("shard", "ctx")),
        P(None, "tp", ("shard", "ctx")),
        P(None, ("shard", "ctx"), "tp"),
        P(None, "tp", ("shard", "ctx")),
        P(None, "tp", ("shard", "ctx")),
        P(None, None, ("shard", "ctx")),
        P(None, None, ("shard", "ctx")),
        P("shard", "ctx", None),
    )
    out_specs = (
        P("shard", "ctx", None),
        P("shard", "ctx", None),
        P(None, None, ("shard", "ctx"), "tp"),
        P(None, None, "tp", ("shard", "ctx")),
        P(None, "tp", ("shard", "ctx")),
        P(None, ("shard", "ctx"), "tp"),
        P(None, "tp", ("shard", "ctx")),
        P(None, "tp", ("shard", "ctx")),
        P(None, None, ("shard", "ctx")),
        P(None, None, ("shard", "ctx")),
    )
    sizes = (mesh.shape["shard"], mesh.shape["ctx"], mesh.shape["tp"])
    return jax.shard_map(
        functools.partial(shards, sizes),
        mesh=mesh,
        in_specs=in_specs,
        out_specs=out_specs,
        check_vma=False,
    )
```
